1024 devices in a mesh: section: 16 (over x, y_lo), expert: 64 (over z, y_hi, core).
Axes of the slice: x: 4, y: 8 (y_hi: 2, y_lo: 4; y = y_hi * 4 + y_lo), z: 16, core: 2. Of those that a mesh axis runs over, the one named last changes fastest.
Arguments:
- forward_handoff: bfloat16 [16, 1024, 3584], P('section', 'expert'), may hold values from -6 to 6
- backward_handoff: bfloat16 [16, 1024, 3584], P('section', 'expert'), may hold values from -6 to 6
- forward_routes: int32 [16, 1024, 2], P('section', 'expert'), may hold values from 0 to 7, all different within a row; in each aligned block of 16 rows (0 to 15, 16 to 31, ..., all dimensions but the last counted through in order) at most 4 rows name the same one
- backward_routes: int32 [16, 1024, 2], P('section', 'expert'), may hold values from 0 to 7, all different within a row; in each aligned block of 16 rows (0 to 15, 16 to 31, ..., all dimensions but the last counted through in order) at most 4 rows name the same one
- forward_gates: float32 [16, 1024, 2], P('section', 'expert'), may hold values from 0.2 to 1.4
- backward_gates: float32 [16, 1024, 2], P('section', 'expert'), may hold values from 0.2 to 1.4
- gate_weight: bfloat16 [16, 3584, 8192], P('section', None, 'expert'), may hold values from -0.09375 to 0.09375
- up_weight: bfloat16 [16, 3584, 8192], P('section', None, 'expert'), may hold values from -0.09375 to 0.09375
- down_weight: bfloat16 [16, 8192, 3584], P('section', 'expert'), may hold values from -0.1875 to 0.1875
- saved_gate: bfloat16 [16, 256, 8192], P('section', None, 'expert'), may hold values from -5 to 5
- saved_up: bfloat16 [16, 256, 8192], P('section', None, 'expert'), may hold values from -5 to 5
Outputs:
- forward_out: bfloat16 [16, 1024, 3584], P('section', 'expert')
- backward_out: bfloat16 [16, 1024, 3584], P('section', 'expert')
The draws below stay inside these ranges and needn't reach their ends.
Inputs may be any that keep to these rules, and one draw needn't show every extreme that they name: `forward_routes`: each token names 2 different experts. In the rows of one index of expert (aligned blocks of 16 tokens) no expert is named more than 4 times, and some block names some expert exactly 4 times. `backward_routes`: each token names 2 different experts. In the rows of one index of expert (aligned blocks of 16 tokens) no expert is named more than 4 times, and some block names some expert exactly 4 times.
All inputs are finite; a program needn't handle non-finite values.
Results may differ from the reference program's by a relative error of at most 0.0054.
Values may be sent and summed in bfloat16 or wider, within the bound.
No kernel may reach another device: no remote copies, remote signals or barrier semaphores. Data moves between devices by JAX's collectives and lax.ppermute only.
A program may use at most 64 MiB of HBM per device.

```python
import math
import jax
import jax.numpy as jnp
import numpy as np
from jax import lax

D = 3584
FE = 1024
EXPERTS = 8
TOPK = 2
TOK_DEV = 16
SHARDS = 8
CAP = 4
SECTIONS = 16
MB = 1024
SLOTS = 256
FEALL = 8192


def levels(own_key, shape, cuts, low, top_value):
    def one(dim, blocks):
        steps = jax.random.uniform(jax.random.fold_in(jax.random.fold_in(own_key, 6), dim), (blocks,), jnp.float32, low / len(cuts), top_value / len(cuts))
        return jnp.repeat(jnp.exp(steps), shape[dim] // blocks).reshape((-1,) + (1,) * (len(shape) - dim - 1))

    loudness = one(*cuts[0])
    for cut in cuts[1:]:
        loudness = loudness * one(*cut)
    return loudness


def routed_block(stream_key, own, number, rows, number_of, top, bound, skew):
    order = jax.random.permutation(stream_key, number_of)
    packed, ordinary = load_shares(number_of, rows * top, bound, skew, True), load_shares(number_of, rows * top, bound, skew, False)
    places = jnp.arange(number_of)

    def named(sizes, rotation):
        used = int((sizes > 0).sum())
        fixed = max(1, used // 4)
        passed = fixed + (places - fixed + rotation * (used - fixed)) % max(1, number_of - fixed)
        return jnp.zeros((number_of,), jnp.int32).at[order[jnp.where(places < fixed, places, passed)]].set(jnp.asarray(sizes, jnp.int32))

    sizes = jnp.where(number % 4 == 0, named(packed, number // 4), named(ordinary, number - number // 4 - 1))
    mixed = jax.random.permutation(jax.random.fold_in(own, 3), number_of)
    donor, receiver = mixed[0:number_of // 2 * 2:2], mixed[1:number_of // 2 * 2:2]
    room = jnp.minimum(sizes[donor] - 1, bound - sizes[receiver]) // 2
    room = jnp.where((donor == order[0]) | (receiver == order[0]) | (sizes[receiver] == 0), 0, jnp.maximum(room, 0))
    passed = jax.random.randint(jax.random.fold_in(own, 4), (number_of // 2,), 0, 1 << 20) % (room + 1)
    sizes = sizes.at[donor].add(-passed).at[receiver].add(passed)
    labels = jnp.searchsorted(jnp.cumsum(sizes), jnp.arange(rows * top), side="right").astype(jnp.int32)
    table = labels.reshape(top, rows).T
    table = table[jax.random.permutation(jax.random.fold_in(own, 1), rows)]
    rotation = jax.random.randint(jax.random.fold_in(own, 2), (rows, 1), 0, top)
    return jnp.take_along_axis(table, (jnp.arange(top)[None, :] + rotation) % top, axis=1)


def load_shares(amount, total, reach, slope, full):
    portions = [(1 << 20) // math.isqrt(grade ** slope) + 1 for grade in range(1, amount + 1)]
    largest = reach if full else min(reach, max(-(-total // amount), total * portions[0] // sum(portions)))
    least = 1 if total - largest >= amount - 1 else 0
    counts, rest = [largest] + [least] * (amount - 1), total - largest - least * (amount - 1)
    while rest > 0:
        candidates = [i for i in range(1, amount) if counts[i] < largest] or [i for i in range(1, amount) if counts[i] < reach]
        whole, remaining = sum([portions[i] for i in candidates]), rest
        for i in candidates:
            addition = min(reach - counts[i], max(1, remaining * portions[i] // whole), rest)
            counts[i] = counts[i] + addition
            rest = rest - addition
    return np.array(counts)


def normal_values(rng, dims, deviation, bound, cuts=(), held_as=jnp.bfloat16):
    level = levels(rng, dims, cuts, -0.22, 0.18) if cuts else 1.0
    drawn = jax.random.normal(rng, dims, jnp.float32) * deviation * level
    return jnp.minimum(jnp.maximum(drawn, -bound), bound).astype(held_as)


def setup_inputs(seed: int = 0) -> dict:
    streams_of = jax.random.split(jax.random.key(seed), 12)
    forward_handoff = normal_values(streams_of[0], (SECTIONS, MB, D), 1.0, 6.0, ((0, 16), (1, 64)))
    backward_handoff = normal_values(streams_of[1], (SECTIONS, MB, D), 1.0, 6.0, ((0, 16), (1, 64)))
    forward_routes_keys = jax.random.split(jax.random.fold_in(streams_of[2], 1), SECTIONS * MB // TOK_DEV)
    forward_routes_turns = jax.random.permutation(jax.random.fold_in(streams_of[2], 3), SECTIONS * MB // TOK_DEV)
    forward_routes = jax.vmap(lambda own, number: routed_block(jax.random.fold_in(streams_of[2], 2), own, number, TOK_DEV, EXPERTS, TOPK, CAP, 1))(forward_routes_keys, forward_routes_turns).reshape((SECTIONS, MB, TOPK))
    backward_routes_keys = jax.random.split(jax.random.fold_in(streams_of[3], 1), SECTIONS * MB // TOK_DEV)
    backward_routes_turns = jax.random.permutation(jax.random.fold_in(streams_of[3], 3), SECTIONS * MB // TOK_DEV)
    backward_routes = jax.vmap(lambda own, number: routed_block(jax.random.fold_in(streams_of[3], 2), own, number, TOK_DEV, EXPERTS, TOPK, CAP, 1))(backward_routes_keys, backward_routes_turns).reshape((SECTIONS, MB, TOPK))
    forward_gates = jnp.clip(0.2 + 1.19999997 * jax.random.uniform(streams_of[4], (SECTIONS, MB, TOPK), jnp.float32) ** levels(streams_of[4], (SECTIONS, MB, TOPK), ((0, 16), (1, 64)), -0.2, 0.2), 0.2, 1.4)
    backward_gates = jnp.clip(0.2 + 1.19999997 * jax.random.uniform(streams_of[5], (SECTIONS, MB, TOPK), jnp.float32) ** levels(streams_of[5], (SECTIONS, MB, TOPK), ((0, 16), (1, 64)), -0.2, 0.2), 0.2, 1.4)
    gate_weight = normal_values(streams_of[6], (SECTIONS, D, FEALL), D ** -0.5, 0.09375, ((0, 16), (2, 64)))
    up_weight = normal_values(streams_of[7], (SECTIONS, D, FEALL), D ** -0.5, 0.09375, ((0, 16), (2, 64)))
    down_weight = normal_values(streams_of[8], (SECTIONS, FEALL, D), FE ** -0.5, 0.1875, ((0, 16), (1, 64)))
    saved_gate = normal_values(streams_of[9], (SECTIONS, SLOTS, FEALL), 1.0, 5.0, ((0, 16), (2, 64)))
    saved_up = normal_values(streams_of[10], (SECTIONS, SLOTS, FEALL), 1.0, 5.0, ((0, 16), (2, 64)))
    return {"forward_handoff": forward_handoff, "backward_handoff": backward_handoff, "forward_routes": forward_routes, "backward_routes": backward_routes, "forward_gates": forward_gates, "backward_gates": backward_gates, "gate_weight": gate_weight, "up_weight": up_weight, "down_weight": down_weight, "saved_gate": saved_gate, "saved_up": saved_up}


def slot_tables(routes, gates):
    count_all = routes.shape[0]
    blocks = count_all // TOK_DEV
    expert_ids = jnp.arange(EXPERTS, dtype=jnp.int32)
    chosen = (routes[:, :, None] == expert_ids[None, None, :]).astype(jnp.float32)
    chosen_any = jnp.sum(chosen, axis=1)
    grouped = chosen_any.reshape(blocks, TOK_DEV, EXPERTS)
    position = jnp.cumsum(grouped, axis=1) - grouped
    slot_ids = jnp.arange(CAP, dtype=jnp.float32)
    placed = (position[..., None] == slot_ids) * grouped[..., None]
    identity = jnp.eye(blocks, dtype=jnp.float32)
    selector = jnp.einsum('btec,bj->ejcbt', placed, identity)
    selector = selector.reshape(EXPERTS, blocks * CAP, blocks * TOK_DEV)
    weighting = jnp.einsum('tk,tke->te', gates, chosen)
    return selector, weighting


def round_hold(values):
    return lax.optimization_barrier(values.astype(jnp.bfloat16)).astype(jnp.float32)


def section_work(inputs):
    (arrive, grad, fwd_routes, bwd_routes, fwd_gates, bwd_gates,
     gate_w, up_w, down_w, kept_gate, kept_up) = inputs
    shards = SHARDS
    width = FE // shards
    high = lax.Precision.HIGHEST
    selector, weighting = slot_tables(fwd_routes, fwd_gates)
    total = arrive.astype(jnp.float32)
    for expert in range(EXPERTS):
        lower = expert * FE
        sent = jnp.dot(selector[expert].astype(jnp.bfloat16), arrive, preferred_element_type=jnp.float32).astype(jnp.bfloat16)
        pre_gate = jnp.dot(sent, gate_w[:, lower:lower + FE], preferred_element_type=jnp.float32)
        pre_up = jnp.dot(sent, up_w[:, lower:lower + FE], preferred_element_type=jnp.float32)
        hidden = (jax.nn.silu(pre_gate) * pre_up).astype(jnp.bfloat16)
        pieces = jnp.einsum('swf,wfd->wsd', hidden.reshape(-1, shards, width).astype(jnp.float32),
                            down_w[lower:lower + FE].reshape(shards, width, D).astype(jnp.float32), precision=high)
        summed = jnp.sum(round_hold(pieces), axis=0)
        back = jnp.dot(selector[expert].T, summed, precision=high)
        total = total + weighting[:, expert:expert + 1] * back
    forward_out = total.astype(jnp.bfloat16)
    selector, weighting = slot_tables(bwd_routes, bwd_gates)
    total = grad.astype(jnp.float32)
    for expert in range(EXPERTS):
        lower = expert * FE
        scaled = (weighting[:, expert:expert + 1] * grad.astype(jnp.float32)).astype(jnp.bfloat16)
        sent = jnp.dot(selector[expert].astype(jnp.bfloat16), scaled, preferred_element_type=jnp.float32).astype(jnp.bfloat16)
        grad_hidden = jnp.dot(sent, down_w[lower:lower + FE].T, preferred_element_type=jnp.float32)
        gate_in = kept_gate[:, lower:lower + FE].astype(jnp.float32)
        up_in = kept_up[:, lower:lower + FE].astype(jnp.float32)
        sigma = jax.nn.sigmoid(gate_in)
        d_gate = (grad_hidden * up_in * sigma * (1.0 + gate_in * (1.0 - sigma))).astype(jnp.bfloat16)
        d_up = (grad_hidden * gate_in * sigma).astype(jnp.bfloat16)
        pieces = jnp.einsum('swf,dwf->wsd', d_gate.reshape(-1, shards, width).astype(jnp.float32),
                            gate_w[:, lower:lower + FE].reshape(D, shards, width).astype(jnp.float32), precision=high)
        pieces = pieces + jnp.einsum('swf,dwf->wsd', d_up.reshape(-1, shards, width).astype(jnp.float32),
                                     up_w[:, lower:lower + FE].reshape(D, shards, width).astype(jnp.float32), precision=high)
        summed = jnp.sum(round_hold(pieces), axis=0)
        total = total + jnp.dot(selector[expert].T, summed, precision=high)
    backward_out = total.astype(jnp.bfloat16)
    return forward_out, backward_out


def reference(forward_handoff, backward_handoff, forward_routes, backward_routes, forward_gates, backward_gates,
              gate_weight, up_weight, down_weight, saved_gate, saved_up):
    arrive = jnp.roll(forward_handoff, 1, axis=0)
    grad = jnp.roll(backward_handoff, -1, axis=0)
    outputs = lax.map(section_work, (arrive, grad, forward_routes, backward_routes, forward_gates, backward_gates,
                                   gate_weight, up_weight, down_weight, saved_gate, saved_up))
    return outputs[0], outputs[1]
```

```python
import jax
import jax.numpy as jnp
import numpy as np
from jax import lax
from jax.sharding import PartitionSpec as P

EXPERTS = 8
CHUNKS = 1
CORE, Y_HI, Z_LO = 1, 2, 4


def from_behind(x, axis, by):
    count = lax.axis_size(axis)
    return lax.ppermute(x, axis, [(i, (i + by) % count) for i in range(count)])


def swap(x, bit):
    count = lax.axis_size("expert")
    return lax.ppermute(x, "expert", [(i, i ^ bit) for i in range(count)])


def across_experts(x, shards):
    groups = [[e * shards + w for e in range(EXPERTS)] for w in range(shards)]
    return lax.all_to_all(
        x, "expert", split_axis=0, concat_axis=0, tiled=True, axis_index_groups=groups
    )


def places(routes, capacity):
    ids = jnp.arange(EXPERTS, dtype=jnp.int32)
    chosen = (routes[:, :, None] == ids).astype(jnp.int32)
    chosen_any = jnp.sum(chosen, axis=1)
    rows = routes.shape[0]
    before = (jnp.arange(rows)[:, None] > jnp.arange(rows)[None, :]).astype(jnp.int32)
    position = jnp.sum(before[:, :, None] * chosen_any[None], axis=1)
    placed = (position[:, :, None] == jnp.arange(capacity, dtype=jnp.int32)).astype(jnp.int32)
    return [chosen[:, k, :, None] * placed for k in range(routes.shape[1])]


def saved_slots(own, shards, capacity):
    rows = []
    per = EXPERTS // CHUNKS
    for part in range(CHUNKS):
        for peer in (0, Y_HI, Z_LO, Y_HI | Z_LO):
            for e in range(part * per, (part + 1) * per):
                for back in (0, 1):
                    for c in range(capacity):
                        rows.append((peer, e, back, c))
    peer, e, back, c = (jnp.asarray(x, jnp.int32) for x in np.array(rows).T)
    return (e * shards + ((own % shards) ^ peer)) * capacity + c, back


def on_device(
    forward_handoff,
    backward_handoff,
    forward_routes,
    backward_routes,
    forward_gates,
    backward_gates,
    gate_weight,
    up_weight,
    down_weight,
    saved_gate,
    saved_up,
):
    shards = lax.axis_size("expert") // EXPERTS
    own = lax.axis_index("expert")
    capacity = saved_gate.shape[1] // lax.axis_size("expert")
    bf16, f32 = jnp.bfloat16, jnp.float32
    hold = lax.optimization_barrier
    arrive = from_behind(forward_handoff[0], "section", 1)
    grad = from_behind(backward_handoff[0], "section", -1)
    tokens, width = arrive.shape
    tile = 2 * capacity

    fwd = places(forward_routes[0], capacity)
    bwd = places(backward_routes[0], capacity)
    zero = jnp.zeros_like(fwd[0])

    def spread(forward, backward):
        both = jnp.stack([forward, backward], axis=2)
        return both.reshape(tokens, EXPERTS * tile).astype(bf16)

    send_table = jnp.concatenate(
        [spread(fwd[0] + fwd[1], zero), spread(zero, bwd[0]), spread(zero, bwd[1])], axis=0
    )
    back_table = jnp.concatenate(
        [spread(fwd[0], zero), spread(fwd[1], zero), spread(zero, bwd[0] + bwd[1])], axis=0
    )
    send_table, back_table = hold((send_table, back_table))

    grad_wide = grad.astype(f32)
    scaled = [(backward_gates[0][:, k : k + 1] * grad_wide).astype(bf16) for k in range(2)]
    rows_in = jnp.concatenate([arrive] + scaled, axis=0)
    first = (((0,), (0,)), ((), ()))
    send = lax.dot_general(send_table, rows_in, first, preferred_element_type=f32).astype(bf16)

    send, gate_local, up_local, down_local, both_saved = hold(
        (
            send,
            gate_weight[0],
            up_weight[0],
            down_weight[0],
            jnp.concatenate([saved_gate[0], saved_up[0]], axis=1),
        )
    )
    got = across_experts(send, shards)
    count = got.shape[0] // CHUNKS

    units = down_local.shape[0]
    weights = hold(jnp.concatenate([gate_local, up_local, down_local.T], axis=1))
    weights = [weights, swap(weights, CORE)]

    def saved_for(device):
        slot, is_back = saved_slots(device, shards, capacity)
        pick = (slot[:, None] == jnp.arange(saved_gate.shape[1])) & (is_back[:, None] == 1)
        return jnp.dot(pick.astype(bf16), both_saved, preferred_element_type=f32).astype(bf16)

    saved = [saved_for(own), swap(saved_for(own ^ CORE), CORE)]
    slopes = []
    for pair in saved:
        g, u = pair[:, :units].astype(f32), pair[:, units:].astype(f32)
        sigma = jax.nn.sigmoid(g)
        slopes.append(hold((u * sigma * (1.0 + g * (1.0 - sigma)), g * sigma)))

    def results(rows, part):
        n = rows.shape[0]
        at = slice(part * n, (part + 1) * n)
        of_forward = (lax.broadcasted_iota(jnp.int32, (n, units), 0) // capacity) % 2 == 0
        last = (((1,), (1,)), ((), ()))
        total = None
        for weight, (slope_gate, slope_up) in zip(weights, slopes):
            pre = jnp.dot(rows, weight, preferred_element_type=f32)
            h = jnp.where(of_forward, jax.nn.silu(pre[:, :units]) * pre[:, units : 2 * units], 0.0)
            dh = pre[:, 2 * units :]
            columns = [dh * slope_gate[at], dh * slope_up[at], h]
            hidden = hold(jnp.concatenate([x.astype(bf16) for x in columns], axis=1))
            term = lax.dot_general(hidden, weight, last, preferred_element_type=f32)
            total = term if total is None else total + term
        return total

    at_z = swap(got, Z_LO)
    near = []
    for part in range(CHUNKS):
        own_rows = slice(part * count, (part + 1) * count)
        at_y = swap(got[own_rows], Y_HI)
        at_zy = swap(at_y, Z_LO)
        near.append(jnp.concatenate([got[own_rows], at_y, at_z[own_rows], at_zy], axis=0))

    done = []
    for part, rows in enumerate(near):
        here = results(rows, part)
        at = [here[i * count : (i + 1) * count] for i in range(4)]
        from_zy = swap(at[3].astype(bf16), Z_LO)
        from_y = swap((at[1] + from_zy.astype(f32)).astype(bf16), Y_HI)
        from_z = swap(at[2].astype(bf16), Z_LO)
        done.append((at[0] + from_z.astype(f32) + from_y.astype(f32)).astype(bf16))
    back = across_experts(jnp.concatenate(done, axis=0), shards)
    sums = jnp.dot(back_table, back, preferred_element_type=f32)
    gates = forward_gates[0]
    forward_out = (
        arrive.astype(f32)
        + gates[:, 0:1] * sums[:tokens]
        + gates[:, 1:2] * sums[tokens : 2 * tokens]
    )
    backward_out = grad_wide + sums[2 * tokens :]
    return (forward_out.astype(bf16)[None], backward_out.astype(bf16)[None])


def solution(mesh):
    return jax.shard_map(
        on_device,
        mesh=mesh,
        in_specs=(
            P("section", "expert", None),
            P("section", "expert", None),
            P("section", "expert", None),
            P("section", "expert", None),
            P("section", "expert", None),
            P("section", "expert", None),
            P("section", None, "expert"),
            P("section", None, "expert"),
            P("section", "expert", None),
            P("section", None, "expert"),
            P("section", None, "expert"),
        ),
        out_specs=(P("section", "expert", None), P("section", "expert", None)),
        check_vma=False,
    )
```

```python
import functools

import jax
import jax.numpy as jnp
import numpy as np
from jax import lax
from jax.experimental import pallas as pl
from jax.experimental.pallas import tpu as pltpu
from jax.sharding import PartitionSpec as P

EXPERTS = 8
CORE, Y_HI, Z_LO = 1, 2, 4
COLUMNS = 512


def from_behind(x, axis, by):
    count = lax.axis_size(axis)
    return lax.ppermute(x, axis, [(i, (i + by) % count) for i in range(count)])


def swap(x, bit):
    count = lax.axis_size("expert")
    return lax.ppermute(x, "expert", [(i, i ^ bit) for i in range(count)])


def across_experts(x, shards):
    groups = [[e * shards + w for e in range(EXPERTS)] for w in range(shards)]
    return lax.all_to_all(
        x, "expert", split_axis=0, concat_axis=0, tiled=True, axis_index_groups=groups
    )


def places(routes, capacity):
    ids = jnp.arange(EXPERTS, dtype=jnp.int32)
    chosen = (routes[:, :, None] == ids).astype(jnp.int32)
    chosen_any = jnp.sum(chosen, axis=1)
    rows = routes.shape[0]
    before = (jnp.arange(rows)[:, None] > jnp.arange(rows)[None, :]).astype(jnp.int32)
    position = jnp.sum(before[:, :, None] * chosen_any[None], axis=1)
    placed = (position[:, :, None] == jnp.arange(capacity, dtype=jnp.int32)).astype(jnp.int32)
    return [chosen[:, k, :, None] * placed for k in range(routes.shape[1])]


def saved_slots(own, shards, capacity):
    rows = [
        (peer, e, back, c)
        for peer in (0, Y_HI, Z_LO, Y_HI | Z_LO)
        for e in range(EXPERTS)
        for back in (0, 1)
        for c in range(capacity)
    ]
    peer, e, back, c = (jnp.asarray(x, jnp.int32) for x in np.array(rows).T)
    return (e * shards + ((own % shards) ^ peer)) * capacity + c, back


def expert_kernel(blocks, capacity, *refs):
    sources, gates, ups, downs = refs[:blocks], *(refs[blocks + i : blocks + i + 2] for i in (0, 2, 4))
    slope_gate, slope_up = refs[blocks + 6 : blocks + 8]
    outs = refs[blocks + 8 : 2 * blocks + 8]
    f32, bf16 = jnp.float32, jnp.bfloat16
    n, width = sources[0].shape
    units = gates[0].shape[1]
    if blocks == 1:
        rows = sources[0]
    else:
        rows = refs[-1]
        for i, ref in enumerate(sources):
            rows[i * n : (i + 1) * n] = ref[...]
    last = (((1,), (1,)), ((), ()))
    row = lax.broadcasted_iota(jnp.int32, (blocks * n, units), 0)
    of_forward = lax.rem(lax.div(row, capacity), 2) == 0
    hidden, d_gate, d_up = [], [], []
    for i, (gate, up, down) in enumerate(zip(gates, ups, downs)):
        pre_gate = jnp.dot(rows[...], gate[...], preferred_element_type=f32)
        pre_up = jnp.dot(rows[...], up[...], preferred_element_type=f32)
        d_hidden = lax.dot_general(rows[...], down[...], last, preferred_element_type=f32)
        silu = pre_gate / (1.0 + jnp.exp(-pre_gate))
        half = slice(i * units, (i + 1) * units)
        hidden.append(jnp.where(of_forward, silu * pre_up, 0.0).astype(bf16))
        d_gate.append((d_hidden * slope_gate[:, half]).astype(bf16))
        d_up.append((d_hidden * slope_up[:, half]).astype(bf16))
    for at in range(0, width, COLUMNS):
        part = pl.ds(at, COLUMNS)
        result = None
        for i, (gate, up, down) in enumerate(zip(gates, ups, downs)):
            term = jnp.dot(hidden[i], down[:, part], preferred_element_type=f32)
            term += lax.dot_general(d_gate[i], gate[part], last, preferred_element_type=f32)
            term += lax.dot_general(d_up[i], up[part], last, preferred_element_type=f32)
            result = term if result is None else result + term
        for i, ref in enumerate(outs):
            ref[:, part] = result[i * n : (i + 1) * n].astype(ref.dtype)


def through_expert(rows, kinds, weights, slopes, capacity):
    blocks = len(rows)
    n, width = rows[0].shape
    units = weights[0].shape[1]
    vmem = pl.BlockSpec(memory_space=pltpu.VMEM)
    return pl.pallas_call(
        functools.partial(expert_kernel, blocks, capacity),
        out_shape=[jax.ShapeDtypeStruct((n, width), kind) for kind in kinds],
        in_specs=[vmem] * (blocks + 8),
        out_specs=[vmem] * blocks,
        scratch_shapes=[pltpu.VMEM((blocks * n, width), jnp.bfloat16)] if blocks > 1 else [],
        compiler_params=pltpu.CompilerParams(vmem_limit_bytes=32 * 1024 * 1024),
        cost_estimate=pl.CostEstimate(
            flops=24 * blocks * n * width * units,
            bytes_accessed=12 * width * units + 6 * blocks * n * width,
            transcendentals=2 * blocks * n * units,
        ),
    )(*rows, *weights, *slopes)


def on_device(
    forward_handoff,
    backward_handoff,
    forward_routes,
    backward_routes,
    forward_gates,
    backward_gates,
    gate_weight,
    up_weight,
    down_weight,
    saved_gate,
    saved_up,
):
    shards = lax.axis_size("expert") // EXPERTS
    own = lax.axis_index("expert")
    capacity = saved_gate.shape[1] // lax.axis_size("expert")
    bf16, f32 = jnp.bfloat16, jnp.float32
    hold = lax.optimization_barrier
    arrive = from_behind(forward_handoff[0], "section", 1)
    grad = from_behind(backward_handoff[0], "section", -1)
    tokens, width = arrive.shape
    tile = 2 * capacity

    fwd = places(forward_routes[0], capacity)
    bwd = places(backward_routes[0], capacity)
    zero = jnp.zeros_like(fwd[0])

    def spread(forward, backward):
        both = jnp.stack([forward, backward], axis=2)
        return both.reshape(tokens, EXPERTS * tile).astype(bf16)

    send_table = jnp.concatenate(
        [spread(fwd[0] + fwd[1], zero), spread(zero, bwd[0]), spread(zero, bwd[1])], axis=0
    )
    back_table = jnp.concatenate(
        [spread(fwd[0], zero), spread(fwd[1], zero), spread(zero, bwd[0] + bwd[1])], axis=0
    )
    send_table, back_table = hold((send_table, back_table))

    grad_wide = grad.astype(f32)
    scaled = [(backward_gates[0][:, k : k + 1] * grad_wide).astype(bf16) for k in range(2)]
    rows_in = jnp.concatenate([arrive] + scaled, axis=0)
    first = (((0,), (0,)), ((), ()))
    send = lax.dot_general(send_table, rows_in, first, preferred_element_type=f32).astype(bf16)

    got = across_experts(send, shards)

    got, gate, up, down, both_saved = hold(
        (
            got,
            gate_weight[0],
            up_weight[0],
            down_weight[0],
            jnp.concatenate([saved_gate[0], saved_up[0]], axis=1),
        )
    )

    weights = [w for mine in (gate, up, down) for w in (mine, swap(mine, CORE))]

    def saved_for(device):
        slot, is_back = saved_slots(device, shards, capacity)
        pick = (slot[:, None] == jnp.arange(saved_gate.shape[1])) & (is_back[:, None] == 1)
        return jnp.dot(pick.astype(bf16), both_saved, preferred_element_type=f32).astype(bf16)

    saved = [saved_for(own), swap(saved_for(own ^ CORE), CORE)]
    g, u = (
        jnp.concatenate([x.astype(f32) for x in pair], axis=1)
        for pair in zip(*(jnp.split(x, 2, axis=1) for x in saved))
    )
    sigma = jax.nn.sigmoid(g)
    slopes = hold((u * sigma * (1.0 + g * (1.0 - sigma)), g * sigma))

    at_y = swap(got, Y_HI)
    at_z = swap(got, Z_LO)
    at_y, at_z = hold((at_y, at_z))
    at_zy = swap(at_y, Z_LO)
    split = 3 * got.shape[0]
    here, to_y, to_z = through_expert(
        [got, at_y, at_z], [f32, f32, bf16], weights, [x[:split] for x in slopes], capacity
    )
    (to_zy,) = through_expert([at_zy], [bf16], weights, [x[split:] for x in slopes], capacity)
    from_zy = swap(to_zy, Z_LO)
    from_y = swap((to_y + from_zy.astype(f32)).astype(bf16), Y_HI)
    from_z = swap(to_z, Z_LO)
    done = (here + from_z.astype(f32) + from_y.astype(f32)).astype(bf16)
    done, arrive, grad, gates, back_table = hold(
        (done, arrive, grad, forward_gates[0], back_table)
    )
    grad_wide = grad.astype(f32)
    back = across_experts(done, shards)
    sums = jnp.dot(back_table, back, preferred_element_type=f32)
    forward_out = (
        arrive.astype(f32)
        + gates[:, 0:1] * sums[:tokens]
        + gates[:, 1:2] * sums[tokens : 2 * tokens]
    )
    backward_out = grad_wide + sums[2 * tokens :]
    return (forward_out.astype(bf16)[None], backward_out.astype(bf16)[None])


def solution(mesh):
    return jax.shard_map(
        on_device,
        mesh=mesh,
        in_specs=(
            P("section", "expert", None),
            P("section", "expert", None),
            P("section", "expert", None),
            P("section", "expert", None),
            P("section", "expert", None),
            P("section", "expert", None),
            P("section", None, "expert"),
            P("section", None, "expert"),
            P("section", "expert", None),
            P("section", None, "expert"),
            P("section", None, "expert"),
        ),
        out_specs=(P("section", "expert", None), P("section", "expert", None)),
        check_vma=False,
    )
```

```python
import functools

import jax
import jax.numpy as jnp
import numpy as np
from jax import lax
from jax.experimental import pallas as pl
from jax.experimental.pallas import tpu as pltpu
from jax.sharding import PartitionSpec as P

EXPERTS = 8
CORE, Y_HI, Z_LO = 1, 2, 4
COLUMNS = 512


def from_behind(x, axis, by):
    count = lax.axis_size(axis)
    return lax.ppermute(x, axis, [(i, (i + by) % count) for i in range(count)])


def swap(x, bit):
    count = lax.axis_size("expert")
    return lax.ppermute(x, "expert", [(i, i ^ bit) for i in range(count)])


def across_experts(x, shards):
    groups = [[e * shards + w for e in range(EXPERTS)] for w in range(shards)]
    return lax.all_to_all(
        x, "expert", split_axis=0, concat_axis=0, tiled=True, axis_index_groups=groups
    )


def places(routes, capacity):
    ids = jnp.arange(EXPERTS, dtype=jnp.int32)
    chosen = (routes[:, :, None] == ids).astype(jnp.int32)
    chosen_any = jnp.sum(chosen, axis=1)
    rows = routes.shape[0]
    before = (jnp.arange(rows)[:, None] > jnp.arange(rows)[None, :]).astype(jnp.int32)
    position = jnp.sum(before[:, :, None] * chosen_any[None], axis=1)
    placed = (position[:, :, None] == jnp.arange(capacity, dtype=jnp.int32)).astype(jnp.int32)
    return [chosen[:, k, :, None] * placed for k in range(routes.shape[1])]


def saved_slots(own, shards, capacity):
    rows = [
        (peer, e, back, c)
        for peer in (0, Y_HI, Z_LO, Y_HI | Z_LO)
        for e in range(EXPERTS)
        for back in (0, 1)
        for c in range(capacity)
    ]
    peer, e, back, c = (jnp.asarray(x, jnp.int32) for x in np.array(rows).T)
    return (e * shards + ((own % shards) ^ peer)) * capacity + c, back


def expert_kernel(blocks, capacity, *refs):
    sources, gates, ups, downs = refs[:blocks], *(refs[blocks + i : blocks + i + 2] for i in (0, 2, 4))
    slope_gate, slope_up = refs[blocks + 6 : blocks + 8]
    outs = refs[blocks + 8 : 2 * blocks + 8]
    f32, bf16 = jnp.float32, jnp.bfloat16
    n, width = sources[0].shape
    units = gates[0].shape[1]
    if blocks == 1:
        rows = sources[0]
    else:
        rows = refs[-1]
        for i, ref in enumerate(sources):
            rows[i * n : (i + 1) * n] = ref[...]
    last = (((1,), (1,)), ((), ()))
    row = lax.broadcasted_iota(jnp.int32, (blocks * n, units), 0)
    of_forward = lax.rem(lax.div(row, capacity), 2) == 0
    hidden, d_gate, d_up = [], [], []
    for i, (gate, up, down) in enumerate(zip(gates, ups, downs)):
        pre_gate = jnp.dot(rows[...], gate[...], preferred_element_type=f32)
        pre_up = jnp.dot(rows[...], up[...], preferred_element_type=f32)
        d_hidden = lax.dot_general(rows[...], down[...], last, preferred_element_type=f32)
        silu = pre_gate / (1.0 + jnp.exp(-pre_gate))
        half = slice(i * units, (i + 1) * units)
        hidden.append(jnp.where(of_forward, silu * pre_up, 0.0).astype(bf16))
        d_gate.append((d_hidden * slope_gate[:, half]).astype(bf16))
        d_up.append((d_hidden * slope_up[:, half]).astype(bf16))
    for at in range(0, width, COLUMNS):
        part = pl.ds(at, COLUMNS)
        result = None
        for i, (gate, up, down) in enumerate(zip(gates, ups, downs)):
            term = jnp.dot(hidden[i], down[:, part], preferred_element_type=f32)
            term += lax.dot_general(d_gate[i], gate[part], last, preferred_element_type=f32)
            term += lax.dot_general(d_up[i], up[part], last, preferred_element_type=f32)
            result = term if result is None else result + term
        for i, ref in enumerate(outs):
            ref[:, part] = result[i * n : (i + 1) * n].astype(ref.dtype)


def through_expert(rows, kinds, weights, slopes, capacity):
    blocks = len(rows)
    n, width = rows[0].shape
    units = weights[0].shape[1]
    vmem = pl.BlockSpec(memory_space=pltpu.VMEM)
    return pl.pallas_call(
        functools.partial(expert_kernel, blocks, capacity),
        out_shape=[jax.ShapeDtypeStruct((n, width), kind) for kind in kinds],
        in_specs=[vmem] * (blocks + 8),
        out_specs=[vmem] * blocks,
        scratch_shapes=[pltpu.VMEM((blocks * n, width), jnp.bfloat16)] if blocks > 1 else [],
        compiler_params=pltpu.CompilerParams(vmem_limit_bytes=32 * 1024 * 1024),
        cost_estimate=pl.CostEstimate(
            flops=24 * blocks * n * width * units,
            bytes_accessed=12 * width * units + 6 * blocks * n * width,
            transcendentals=2 * blocks * n * units,
        ),
    )(*rows, *weights, *slopes)


def on_device(
    forward_handoff,
    backward_handoff,
    forward_routes,
    backward_routes,
    forward_gates,
    backward_gates,
    gate_weight,
    up_weight,
    down_weight,
    saved_gate,
    saved_up,
):
    shards = lax.axis_size("expert") // EXPERTS
    own = lax.axis_index("expert")
    capacity = saved_gate.shape[1] // lax.axis_size("expert")
    bf16, f32 = jnp.bfloat16, jnp.float32
    hold = lax.optimization_barrier
    arrive = from_behind(forward_handoff[0], "section", 1)
    grad = from_behind(backward_handoff[0], "section", -1)
    tokens, width = arrive.shape
    tile = 2 * capacity

    fwd = places(forward_routes[0], capacity)
    bwd = places(backward_routes[0], capacity)
    zero = jnp.zeros_like(fwd[0])

    def spread(forward, backward):
        both = jnp.stack([forward, backward], axis=2)
        return both.reshape(tokens, EXPERTS * tile).astype(bf16)

    send_table = jnp.concatenate(
        [spread(fwd[0] + fwd[1], zero), spread(zero, bwd[0]), spread(zero, bwd[1])], axis=0
    )
    back_table = jnp.concatenate(
        [spread(fwd[0], zero), spread(fwd[1], zero), spread(zero, bwd[0] + bwd[1])], axis=0
    )
    send_table, back_table = hold((send_table, back_table))

    grad_wide = grad.astype(f32)
    scaled = [(backward_gates[0][:, k : k + 1] * grad_wide).astype(bf16) for k in range(2)]
    rows_in = jnp.concatenate([arrive] + scaled, axis=0)
    first = (((0,), (0,)), ((), ()))
    send = lax.dot_general(send_table, rows_in, first, preferred_element_type=f32).astype(bf16)

    send, both_saved = hold((send, jnp.concatenate([saved_gate[0], saved_up[0]], axis=1)))
    got = across_experts(send, shards)

    def saved_for(device):
        slot, is_back = saved_slots(device, shards, capacity)
        pick = (slot[:, None] == jnp.arange(saved_gate.shape[1])) & (is_back[:, None] == 1)
        return jnp.dot(pick.astype(bf16), both_saved, preferred_element_type=f32).astype(bf16)

    saved_other = swap(saved_for(own ^ CORE), CORE)
    got, saved_other, gate, up, down = hold(
        (got, saved_other, gate_weight[0], up_weight[0], down_weight[0])
    )
    weights = [w for mine in (gate, up, down) for w in (mine, swap(mine, CORE))]
    saved = [saved_for(own), saved_other]
    g, u = (
        jnp.concatenate([x.astype(f32) for x in pair], axis=1)
        for pair in zip(*(jnp.split(x, 2, axis=1) for x in saved))
    )
    sigma = jax.nn.sigmoid(g)
    slopes = hold((u * sigma * (1.0 + g * (1.0 - sigma)), g * sigma))

    at_y = swap(got, Y_HI)
    at_z = swap(got, Z_LO)
    at_y, at_z = hold((at_y, at_z))
    at_zy = swap(at_y, Z_LO)
    split = 3 * got.shape[0]
    here, to_y, to_z = through_expert(
        [got, at_y, at_z], [f32, f32, bf16], weights, [x[:split] for x in slopes], capacity
    )
    (to_zy,) = through_expert([at_zy], [bf16], weights, [x[split:] for x in slopes], capacity)
    from_zy = swap(to_zy, Z_LO)
    from_y = swap((to_y + from_zy.astype(f32)).astype(bf16), Y_HI)
    from_z = swap(to_z, Z_LO)
    done = (here + from_z.astype(f32) + from_y.astype(f32)).astype(bf16)
    done, arrive, grad, gates, back_table = hold(
        (done, arrive, grad, forward_gates[0], back_table)
    )
    grad_wide = grad.astype(f32)
    back = across_experts(done, shards)
    sums = jnp.dot(back_table, back, preferred_element_type=f32)
    forward_out = (
        arrive.astype(f32)
        + gates[:, 0:1] * sums[:tokens]
        + gates[:, 1:2] * sums[tokens : 2 * tokens]
    )
    backward_out = grad_wide + sums[2 * tokens :]
    return (forward_out.astype(bf16)[None], backward_out.astype(bf16)[None])


def solution(mesh):
    return jax.shard_map(
        on_device,
        mesh=mesh,
        in_specs=(
            P("section", "expert", None),
            P("section", "expert", None),
            P("section", "expert", None),
            P("section", "expert", None),
            P("section", "expert", None),
            P("section", "expert", None),
            P("section", None, "expert"),
            P("section", None, "expert"),
            P("section", "expert", None),
            P("section", None, "expert"),
            P("section", None, "expert"),
        ),
        out_specs=(P("section", "expert", None), P("section", "expert", None)),
        check_vma=False,
    )
```
